32 devices in a mesh: wide: 8 (over z, y), narrow: 4 (over x, core).
Axes of the slice: x: 2, y: 2, z: 4, core: 2. Of those that a mesh axis runs over, the one named last changes fastest.
Arguments:
- hidden: bfloat16 [16384, 8192], P('wide', 'narrow'), may hold values from -6 to 6
- base_key_value: bfloat16 [8192, 8, 2, 128], P('narrow'), may hold values from -0.0625 to 0.0625
- store_a: bfloat16 [64, 8192, 128], P('wide', 'narrow'), may hold values from -0.0625 to 0.0625
- stored_up_maps: bfloat16 [64, 2, 64, 8, 128], P('wide', None, None, 'narrow'), may hold values from -0.75 to 0.75
- adapter_ids: int32 [128], P('wide'), may hold values from 0 to 63, as said below
- span_start: int32 [128], P('wide'), may hold values from 0 to 31
Outputs:
- key_value: bfloat16 [8, 16384, 2, 128], P('narrow', 'wide')
The draws below stay inside these ranges and needn't reach their ends.
Inputs may be any that keep to these rules, and one draw needn't show every extreme that they name: `adapter_ids`: requests of one replica that name different adapters name adapters of different owners, the owner of adapter a being the replica a // 8.
All inputs are finite; a program needn't handle non-finite values.
Results may differ from the reference program's by a relative error of at most 0.015.
Values may be sent and summed in bfloat16 or wider, within the bound.
A program may use at most 192 MiB of HBM per device.

```python
import jax
import jax.numpy as jnp
from jax import lax

MODEL_WIDTH = 8192
KEY_VALUE_HEADS = 8
HEAD_SIZE = 128
ADAPTER_RANK = 64
REQUEST_TOKENS = 128
REPLICA_REQUESTS = 16
ADAPT_DEV = 8
STORED_ADAPTERS = 64
NREQ = 128
TOKENS = 16384
N_WIDE = 8
N_NARROW = 4


def force_front(order, target, place):
    current = order[place]
    moved = jnp.where(order == target, current, order)
    return moved.at[place].set(target)


def draw_adapter_ids(key, part):
    subkeys = jax.random.split(jax.random.fold_in(key, 17), 3)
    row_keys = jax.random.split(subkeys[0], N_WIDE)
    owner_orders = jax.vmap(lambda subkey: jax.random.permutation(subkey, N_WIDE))(row_keys).astype(jnp.int32)
    first_row = force_front(owner_orders[0], jnp.int32(N_WIDE // 2), 0)
    first_row = force_front(first_row, jnp.int32(1), 1)
    second_row = force_front(owner_orders[1], jnp.int32(0), 0)
    owner_orders = owner_orders.at[0].set(first_row).at[1].set(second_row)
    slot_table = jnp.minimum(jax.random.randint(subkeys[1], (N_WIDE, N_WIDE), 0, ADAPT_DEV), jax.random.randint(subkeys[2], (N_WIDE, N_WIDE), 0, ADAPT_DEV))
    positions = jnp.arange(REPLICA_REQUESTS, dtype=jnp.int32) % N_WIDE
    owners = owner_orders[:, positions]
    slot_ids = slot_table[:, positions]
    picked = owners * ADAPT_DEV + slot_ids
    return picked.reshape(N_WIDE * REPLICA_REQUESTS).astype(jnp.int32)


def touch_ends(entries, rng, smallest, high):
    extent = entries.shape
    spot = [jax.random.randint(jax.random.fold_in(rng, axis), (), 0, extent[axis]) for axis in range(len(extent))]
    entries = entries.at[tuple(spot)].set(smallest)
    longest = extent.index(max(extent))
    spot[longest] = (spot[longest] + 1) % extent[longest]
    return entries.at[tuple(spot)].set(high)


def steps_of(own_key, extent, cuts, least, high):
    gain, own = 1.0, jax.random.fold_in(own_key, 6)
    for dim, blocks in cuts:
        steps = jnp.exp(jax.random.uniform(jax.random.fold_in(own, dim), (blocks,), jnp.float32, least / len(cuts), high / len(cuts)))
        gain = gain * jnp.repeat(steps, extent[dim] // blocks).reshape([-1 if axis == dim else 1 for axis in range(len(extent))])
    return gain


def centred(rng, dims, deviation, most, pieces=(), held_as=jnp.bfloat16):
    entries = deviation * jax.random.normal(rng, dims, jnp.float32)
    if pieces:
        entries = entries * steps_of(rng, dims, pieces, -0.22, 0.18)
    return jnp.clip(entries, -most, most).astype(held_as)


def setup_inputs(seed: int = 0) -> dict:
    streams_of = jax.random.split(jax.random.key(seed), 7)
    hidden = centred(streams_of[0], (TOKENS, MODEL_WIDTH), 1.0, 6.0, ((0, 8), (1, 4)))
    base_key_value = centred(streams_of[1], (MODEL_WIDTH, KEY_VALUE_HEADS, 2, HEAD_SIZE), MODEL_WIDTH ** -0.5, 0.0625, ((0, 4),))
    store_a = centred(streams_of[2], (STORED_ADAPTERS, MODEL_WIDTH, 2 * ADAPTER_RANK), MODEL_WIDTH ** -0.5, 0.0625, ((0, 8), (1, 4)))
    stored_up_maps = centred(streams_of[3], (STORED_ADAPTERS, 2, ADAPTER_RANK, KEY_VALUE_HEADS, HEAD_SIZE), ADAPTER_RANK ** -0.5, 0.75, ((0, 8), (3, 4)))
    adapter_ids = draw_adapter_ids(jax.random.fold_in(streams_of[6], 71), 0)
    span_start = touch_ends(jax.random.randint(streams_of[5], (NREQ,), 0, 32), jax.random.fold_in(streams_of[5], 1), 0, 31).astype(jnp.int32)
    return dict(hidden=hidden, base_key_value=base_key_value, store_a=store_a, stored_up_maps=stored_up_maps, adapter_ids=adapter_ids, span_start=span_start)


THETA = 500000.0


def rotate_keys(values, positions):
    half_dim = values.shape[-1] // 2
    frequency = THETA ** (-(jnp.arange(half_dim, dtype=jnp.float32) * 2.0 / values.shape[-1]))
    angles = positions[:, None] * frequency[None, :]
    angles = jnp.concatenate([angles, angles], axis=-1)
    turned = jnp.concatenate([-values[..., half_dim:], values[..., :half_dim]], axis=-1)
    return values * jnp.cos(angles) + turned * jnp.sin(angles)


def reference(hidden, base_key_value, store_a, stored_up_maps, adapter_ids, span_start):
    local_width = MODEL_WIDTH // N_NARROW
    weight_float_copy = base_key_value.astype(jnp.float32).reshape(N_NARROW, local_width, KEY_VALUE_HEADS * 2 * HEAD_SIZE)

    def per_request(request):
        request = request.astype(jnp.int32)
        rows = lax.dynamic_slice_in_dim(hidden, request * REQUEST_TOKENS, REQUEST_TOKENS, 0)
        split_rows = rows.astype(jnp.float32).reshape(REQUEST_TOKENS, N_NARROW, local_width)
        partial_sums = jnp.einsum('tnd,ndc->ntc', split_rows, weight_float_copy)
        partial_sums = lax.optimization_barrier(partial_sums.astype(jnp.bfloat16)).astype(jnp.float32)
        base_total_sum = jnp.sum(partial_sums, axis=0).reshape(REQUEST_TOKENS, KEY_VALUE_HEADS, 2, HEAD_SIZE)
        adapter_a = store_a[adapter_ids[request]]
        adapter_b = stored_up_maps[adapter_ids[request]]
        shrunk = jnp.dot(rows, adapter_a, preferred_element_type=jnp.float32).astype(jnp.bfloat16)
        shrunk = shrunk.reshape(REQUEST_TOKENS, 2, ADAPTER_RANK)
        delta = jnp.einsum('tjk,jkhc->thjc', shrunk.astype(jnp.float32), adapter_b.astype(jnp.float32))
        raw = base_total_sum + delta
        positions = (span_start[request] * REQUEST_TOKENS + jnp.arange(REQUEST_TOKENS, dtype=jnp.int32)).astype(jnp.float32)
        keys_turned = jax.vmap(lambda head_keys: rotate_keys(head_keys, positions), in_axes=1, out_axes=1)(raw[:, :, 0, :])
        joined = jnp.stack([keys_turned, raw[:, :, 1, :]], axis=2)
        return joined.astype(jnp.bfloat16)

    token_blocks = lax.map(per_request, jnp.arange(N_WIDE * REPLICA_REQUESTS, dtype=jnp.int32))
    token_blocks = token_blocks.reshape(N_WIDE * REPLICA_REQUESTS * REQUEST_TOKENS, KEY_VALUE_HEADS, 2, HEAD_SIZE)
    return jnp.transpose(token_blocks, (1, 0, 2, 3))
```

```python
import functools

import jax
import jax.numpy as jnp
from jax import lax
from jax.experimental import pallas as pl
from jax.experimental.pallas import tpu as pltpu
from jax.sharding import PartitionSpec as P

THETA = 500000.0
MESH = pl.DeviceIdType.MESH
F32, BF16 = jnp.float32, jnp.bfloat16


def flip(index, k, bits):
    total = 0
    for b in range(bits):
        bit = lax.rem(index // (1 << b), 2)
        total = total + lax.rem(bit + ((k >> b) & 1), 2) * (1 << b)
    return total


def pick(chosen, a_ref, b_ref, ra_ref, rb_ref):
    ra_ref[...] = a_ref[...]
    rb_ref[...] = b_ref[...]


def main(
    nw, nx, slot_ref, hid_hbm, w_hbm, ra, rb, ca, sa, cb, sb, out,
    hid, w, abuf, bbuf, psend, prec, xsend, xrec, base, acc, s1s, s1r, s2s, s2r, finm, fino,
    lsem, wsem, a_s, a_r, b_s, b_r, p_s, p_r, x_s, x_r, t_s, t_r,
):
    bits = nw.bit_length() - 1
    wi, ni = lax.axis_index("wide"), lax.axis_index("narrow")
    xi, ci = ni // 2, lax.rem(ni, 2)
    tokens, cols = base.shape
    half = tokens // 2
    span = cb.shape[0]
    heads = cols // 256
    partner = (wi, xi * 2 + 1 - ci)
    across = [(wi, lax.rem(xi + d, nx) * 2 + ci) for d in range(1, nx)]
    replicas = [(flip(wi, k, bits), ni) for k in range(1, nw)]

    barrier = pltpu.get_barrier_semaphore()
    for peer in [partner, *across, *replicas]:
        pl.semaphore_signal(barrier, inc=1, device_id=peer, device_id_type=MESH)

    hid_copy = pltpu.make_async_copy(hid_hbm, hid, lsem.at[0])
    hid_copy.start()
    order = [(d, 1) for d in [*range(1, nx), 0]] + [(d, 0) for d in [*range(1, nx), 0]]
    w_copies = []
    for i, (d, other) in enumerate(order):
        core = 1 - ci if other else ci
        block = lax.rem(xi + d, nx) * 2 + core
        w_copies.append(pltpu.make_async_copy(w_hbm.at[block], w.at[i], wsem.at[i]))
        w_copies[-1].start()
    own_a = pltpu.make_async_copy(ra.at[wi], abuf.at[0], lsem.at[1])
    own_b = pltpu.make_async_copy(rb.at[wi], bbuf.at[0], lsem.at[2])
    own_a.start()
    own_b.start()

    pl.semaphore_wait(barrier, nw - 1 + nx)

    def remote(src, dst, s, r, peer):
        return pltpu.make_async_remote_copy(
            src_ref=src, dst_ref=dst, send_sem=s, recv_sem=r, device_id=peer, device_id_type=MESH
        )

    a_copies, b_copies = {}, {}
    for k in [*range(nw // 2, nw), *range(1, nw // 2)]:
        to = replicas[k - 1]
        a_copies[k] = remote(ra.at[to[0]], abuf.at[k], a_s.at[k], a_r.at[k], to)
        b_copies[k] = remote(rb.at[to[0]], bbuf.at[k], b_s.at[k], b_r.at[k], to)
        b_copies[k].start()
        a_copies[k].start()

    tile = 512
    hid_copy.wait()

    def product(i, store):
        w_copies[i].wait()

        def body(t, carry):
            rows = pl.ds(pl.multiple_of(t * tile, tile), tile)
            store(rows, jnp.dot(hid[rows, :], w[i], preferred_element_type=F32))
            return carry

        lax.fori_loop(0, tokens // tile, body, 0)

    p_copies, x_copies = {}, {}
    for i, (d, other) in enumerate(order):
        if other:

            def to_partner(rows, value, d=d):
                psend[d, rows, :] = value.astype(BF16)

            product(i, to_partner)
            p_copies[d] = remote(psend.at[d], prec.at[d], p_s.at[d], p_r.at[d], partner)
            p_copies[d].start()
        elif d:

            def to_across(rows, value, d=d):
                xsend[d - 1, rows, :] = (value + prec[d, rows, :].astype(F32)).astype(BF16)

            p_copies[d].wait()
            product(i, to_across)
            x_copies[d] = remote(xsend.at[d - 1], xrec.at[d - 1], x_s.at[d], x_r.at[d], across[d - 1])
            x_copies[d].start()
        else:

            def to_base(rows, value):
                base[rows, :] = value + prec[0, rows, :].astype(F32)

            p_copies[0].wait()
            product(i, to_base)

    for k in range(0, nw, 2):
        if k:
            a_copies[k].wait()
            a_copies[k + 1].wait()
        else:
            own_a.wait()
            a_copies[1].wait()

        def shrink(t, carry, k=k):
            both = jnp.concatenate([abuf[k], abuf[k + 1]], axis=1)
            rows = pl.ds(pl.multiple_of(t * tile, tile), tile)
            made = jnp.dot(hid[rows, :], both, preferred_element_type=F32)
            for q in range(tile // span):
                slot = slot_ref[t * (tile // span) + q]
                part = pl.ds(pl.multiple_of(t * tile + q * span, span), span)
                mine = made[q * span : (q + 1) * span]
                before = acc[part, :] if k else jnp.zeros((span, 128), F32)
                acc[part, :] = jnp.where(
                    slot == k, mine[:, :128], jnp.where(slot == k + 1, mine[:, 128:], before)
                )
            return carry

        lax.fori_loop(0, tokens // tile, shrink, 0)

    mine0 = pl.multiple_of(ci * half, half)
    other0 = pl.multiple_of((1 - ci) * half, half)
    s1s[...] = acc[pl.ds(other0, half), :].astype(BF16)
    first = remote(s1s, s1r, t_s.at[0], t_r.at[0], partner)
    first.start()
    for d in range(1, nx):
        x_copies[d].wait()
    own_b.wait()
    for k in range(1, nw):
        b_copies[k].wait()
    first.wait()
    summed = acc[pl.ds(mine0, half), :] + s1r[...].astype(F32)
    acc[pl.ds(mine0, half), :] = summed
    s2s[...] = summed.astype(BF16)
    seconds = []
    for d in range(1, nx):
        seconds.append(remote(s2s, s2r.at[d - 1], t_s.at[d], t_r.at[d], across[d - 1]))
        seconds[-1].start()
    for copy in seconds:
        copy.wait()
    total = acc[pl.ds(mine0, half), :]
    for d in range(1, nx):
        total = total + s2r[d - 1].astype(F32)
    finm[...] = total.astype(BF16)
    last = remote(finm, fino, t_s.at[nx], t_r.at[nx], partner)
    last.start()

    def finish(source, row0):
        def body(q, carry):
            rows = pl.ds(pl.multiple_of(row0 + q * span, span), span)
            r = row0 // span + q
            b = bbuf[slot_ref[r]]
            upper = lax.broadcasted_iota(jnp.int32, b.shape, 0) < b.shape[0] // 2
            zero = jnp.zeros_like(b)
            maps = jnp.concatenate([jnp.where(upper, b, zero), jnp.where(upper, zero, b)], axis=1)
            low = source[pl.ds(pl.multiple_of(q * span, span), span), :]
            delta = jnp.dot(low, maps, preferred_element_type=F32)
            raw = base[rows, :]
            for d in range(1, nx):
                raw = raw + xrec[d - 1, rows, :].astype(F32)
            cos_a, sin_a = ca[pl.ds(r, 1), :], sa[pl.ds(r, 1), :]
            cos = cos_a * cb[...] - sin_a * sb[...]
            sin = sin_a * cb[...] + cos_a * sb[...]
            lane = lax.broadcasted_iota(jnp.int32, sin.shape, 1)
            sin = jnp.where(lane < 64, -sin, sin)
            for h in range(heads):
                key = raw[:, h * 256 : h * 256 + 128] + delta[:, h * 128 : (h + 1) * 128]
                value = raw[:, h * 256 + 128 : (h + 1) * 256]
                value = value + delta[:, (heads + h) * 128 : (heads + h + 1) * 128]
                out[h, 0, rows, :] = (key * cos + pltpu.roll(key, 64, 1) * sin).astype(BF16)
                out[h, 1, rows, :] = value.astype(BF16)
            return carry

        lax.fori_loop(0, half // span, body, 0)

    finish(finm, mine0)
    last.wait()
    finish(fino, other0)


def shards(hidden, base_key_value, store_a, stored_up_maps, adapter_ids, span_start):
    nw, nn = lax.axis_size("wide"), lax.axis_size("narrow")
    nx = nn // 2
    stored, features, rank_two = store_a.shape
    requests = adapter_ids.shape[0]
    tokens = hidden.shape[0]
    span = tokens // requests
    cols = base_key_value.shape[1] * 256 // nn
    owners = adapter_ids // stored
    slot_ids = adapter_ids % stored
    matches = owners[None, :] == jnp.arange(nw, dtype=jnp.int32)[:, None]
    wanted = jnp.max(jnp.where(matches, slot_ids[None, :] + 1, 0), axis=1).reshape(nw, 1)
    asked = lax.all_to_all(wanted, "wide", split_axis=0, concat_axis=0, tiled=True)
    chosen = jnp.maximum(asked[:, 0] - 1, 0)
    arrival = owners ^ lax.axis_index("wide").astype(jnp.int32)

    up = stored_up_maps.reshape(stored, rank_two, -1)
    across = up.shape[2]
    ra, rb = pl.pallas_call(
        pick,
        grid_spec=pltpu.PrefetchScalarGridSpec(
            num_scalar_prefetch=1,
            grid=(nw,),
            in_specs=[
                pl.BlockSpec((1, features, rank_two), lambda i, c: (c[i], 0, 0)),
                pl.BlockSpec((1, rank_two, across), lambda i, c: (c[i], 0, 0)),
            ],
            out_specs=[
                pl.BlockSpec((1, features, rank_two), lambda i, c: (i, 0, 0)),
                pl.BlockSpec((1, rank_two, across), lambda i, c: (i, 0, 0)),
            ],
        ),
        out_shape=[
            jax.ShapeDtypeStruct((nw, features, rank_two), BF16),
            jax.ShapeDtypeStruct((nw, rank_two, across), BF16),
        ],
    )(chosen, store_a, up)

    weights = base_key_value.reshape(features, nn, cols).transpose(1, 0, 2)
    frequency = THETA ** (-(jnp.arange(64, dtype=F32) * 2.0 / 128))
    frequency = jnp.concatenate([frequency, frequency])[None, :]
    start = (span_start * span).astype(F32)[:, None] * frequency
    step = jnp.arange(span, dtype=F32)[:, None] * frequency

    vmem, smem, hbm = (pl.BlockSpec(memory_space=m) for m in (pltpu.VMEM, pltpu.SMEM, pl.ANY))
    dma = pltpu.SemaphoreType.DMA
    half = tokens // 2
    heads = cols // 256
    out = pl.pallas_call(
        functools.partial(main, nw, nx),
        out_shape=jax.ShapeDtypeStruct((heads, 2, tokens, 128), BF16),
        in_specs=[smem, hbm, hbm, hbm, hbm, vmem, vmem, vmem, vmem],
        out_specs=vmem,
        scratch_shapes=[
            pltpu.VMEM((tokens, features), BF16),
            pltpu.VMEM((nn, features, cols), BF16),
            pltpu.VMEM((nw, features, rank_two), BF16),
            pltpu.VMEM((nw, rank_two, across), BF16),
            pltpu.VMEM((nx, tokens, cols), BF16),
            pltpu.VMEM((nx, tokens, cols), BF16),
            pltpu.VMEM((nx - 1, tokens, cols), BF16),
            pltpu.VMEM((nx - 1, tokens, cols), BF16),
            pltpu.VMEM((tokens, cols), F32),
            pltpu.VMEM((tokens, rank_two), F32),
            pltpu.VMEM((half, rank_two), BF16),
            pltpu.VMEM((half, rank_two), BF16),
            pltpu.VMEM((half, rank_two), BF16),
            pltpu.VMEM((nx - 1, half, rank_two), BF16),
            pltpu.VMEM((half, rank_two), BF16),
            pltpu.VMEM((half, rank_two), BF16),
            dma((3,)), dma((nn,)), dma((nw,)), dma((nw,)), dma((nw,)), dma((nw,)),
            dma((nx,)), dma((nx,)), dma((nx,)), dma((nx,)), dma((nx + 1,)), dma((nx + 1,)),
        ],
        compiler_params=pltpu.CompilerParams(
            collective_id=0, has_side_effects=True, vmem_limit_bytes=58 * 2**20
        ),
        cost_estimate=pl.CostEstimate(
            flops=2 * tokens * features * 3072, bytes_accessed=2**25, transcendentals=0
        ),
    )(arrival, hidden, weights, ra, rb, jnp.cos(start), jnp.sin(start), jnp.cos(step), jnp.sin(step))
    return out.transpose(0, 2, 1, 3)


def solution(mesh):
    placed = (
        P("wide", "narrow"),
        P("narrow", None, None, None),
        P("wide", "narrow", None),
        P("wide", None, None, "narrow", None),
        P("wide"),
        P("wide"),
    )
    return jax.shard_map(
        shards,
        mesh=mesh,
        in_specs=placed,
        out_specs=P("narrow", "wide", None, None),
        check_vma=False,
    )
```

```python
import functools

import jax
import jax.numpy as jnp
from jax import lax
from jax.experimental import pallas as pl
from jax.experimental.pallas import tpu as pltpu
from jax.sharding import PartitionSpec as P

THETA = 500000.0
MESH = pl.DeviceIdType.MESH
F32, BF16 = jnp.float32, jnp.bfloat16


def flip(index, k, bits):
    total = 0
    for b in range(bits):
        bit = lax.rem(index // (1 << b), 2)
        total = total + lax.rem(bit + ((k >> b) & 1), 2) * (1 << b)
    return total


def main(
    nw, nx, slot_ref, chosen_ref, hid_hbm, w_hbm, store_hbm, up, ca, sa, cb, sb, out,
    hid, raw_w, w, store, ra, rb, abuf, bbuf, psend, prec, xsend, xrec, base, acc, s1s, s1r, s2s, s2r, finm, fino,
    lsem, a_s, a_r, b_s, b_r, p_s, p_r, x_s, x_r, t_s, t_r,
):
    bits = nw.bit_length() - 1
    wi, ni = lax.axis_index("wide"), lax.axis_index("narrow")
    xi, ci = ni // 2, lax.rem(ni, 2)
    tokens, cols = base.shape
    half = tokens // 2
    span = cb.shape[0]
    heads = cols // 256
    partner = (wi, xi * 2 + 1 - ci)
    across = [(wi, lax.rem(xi + d, nx) * 2 + ci) for d in range(1, nx)]
    replicas = [(flip(wi, k, bits), ni) for k in range(1, nw)]

    barrier = pltpu.get_barrier_semaphore()
    for peer in [partner, *across, *replicas]:
        pl.semaphore_signal(barrier, inc=1, device_id=peer, device_id_type=MESH)

    store_copy = pltpu.make_async_copy(store_hbm, store, lsem.at[0])
    store_copy.start()
    w_copy = pltpu.make_async_copy(w_hbm, raw_w, lsem.at[1])
    w_copy.start()
    hid_copy = pltpu.make_async_copy(hid_hbm, hid, lsem.at[2])
    hid_copy.start()
    order = [(d, 1) for d in [*range(1, nx), 0]] + [(d, 0) for d in [*range(1, nx), 0]]
    store_copy.wait()

    pl.semaphore_wait(barrier, nw - 1 + nx)

    def remote(src, dst, s, r, peer):
        return pltpu.make_async_remote_copy(
            src_ref=src, dst_ref=dst, send_sem=s, recv_sem=r, device_id=peer, device_id_type=MESH
        )

    a_copies, b_copies = {}, {}
    for k in [*range(nw // 2, nw), *range(1, nw // 2)]:
        to = replicas[k - 1]
        ra[k] = store[chosen_ref[to[0]]]
        rb[k] = up[chosen_ref[to[0]]]
        a_copies[k] = remote(ra.at[k], abuf.at[k], a_s.at[k], a_r.at[k], to)
        b_copies[k] = remote(rb.at[k], bbuf.at[k], b_s.at[k], b_r.at[k], to)
        b_copies[k].start()
        a_copies[k].start()

    abuf[0] = store[chosen_ref[wi]]
    bbuf[0] = up[chosen_ref[wi]]
    tile = 512
    w_copy.wait()
    hid_copy.wait()

    def product(i, store):
        d, other = order[i]
        block = lax.rem(xi + d, nx) * 2 + (1 - ci if other else ci)
        step = 256

        def unpack(t, carry):
            rows = pl.ds(pl.multiple_of(t * step, step), step)
            for h in range(heads):
                pair = raw_w[rows, block * heads + h].astype(F32)
                for j in range(2):
                    w[rows, (2 * h + j) * 128 : (2 * h + j + 1) * 128] = pair[:, j, :].astype(BF16)
            return carry

        lax.fori_loop(0, w.shape[0] // step, unpack, 0)

        def body(t, carry):
            rows = pl.ds(pl.multiple_of(t * tile, tile), tile)
            store(rows, jnp.dot(hid[rows, :], w[...], preferred_element_type=F32))
            return carry

        lax.fori_loop(0, tokens // tile, body, 0)

    p_copies, x_copies = {}, {}
    for i, (d, other) in enumerate(order):
        if other:

            def to_partner(rows, value, d=d):
                psend[d, rows, :] = value.astype(BF16)

            product(i, to_partner)
            p_copies[d] = remote(psend.at[d], prec.at[d], p_s.at[d], p_r.at[d], partner)
            p_copies[d].start()
        elif d:

            def to_across(rows, value, d=d):
                xsend[d - 1, rows, :] = (value + prec[d, rows, :].astype(F32)).astype(BF16)

            p_copies[d].wait()
            product(i, to_across)
            x_copies[d] = remote(xsend.at[d - 1], xrec.at[d - 1], x_s.at[d], x_r.at[d], across[d - 1])
            x_copies[d].start()
        else:

            def to_base(rows, value):
                base[rows, :] = value + prec[0, rows, :].astype(F32)

            p_copies[0].wait()
            product(i, to_base)

    for k in range(0, nw, 2):
        if k:
            a_copies[k].wait()
            a_copies[k + 1].wait()
        else:
            a_copies[1].wait()

        def shrink(t, carry, k=k):
            both = jnp.concatenate([abuf[k], abuf[k + 1]], axis=1)
            rows = pl.ds(pl.multiple_of(t * tile, tile), tile)
            made = jnp.dot(hid[rows, :], both, preferred_element_type=F32)
            for q in range(tile // span):
                slot = slot_ref[t * (tile // span) + q]
                part = pl.ds(pl.multiple_of(t * tile + q * span, span), span)
                mine = made[q * span : (q + 1) * span]
                before = acc[part, :] if k else jnp.zeros((span, 128), F32)
                acc[part, :] = jnp.where(
                    slot == k, mine[:, :128], jnp.where(slot == k + 1, mine[:, 128:], before)
                )
            return carry

        lax.fori_loop(0, tokens // tile, shrink, 0)

    mine0 = pl.multiple_of(ci * half, half)
    other0 = pl.multiple_of((1 - ci) * half, half)
    s1s[...] = acc[pl.ds(other0, half), :].astype(BF16)
    first = remote(s1s, s1r, t_s.at[0], t_r.at[0], partner)
    first.start()
    for d in range(1, nx):
        x_copies[d].wait()
    for k in range(1, nw):
        b_copies[k].wait()
    first.wait()
    summed = acc[pl.ds(mine0, half), :] + s1r[...].astype(F32)
    acc[pl.ds(mine0, half), :] = summed
    s2s[...] = summed.astype(BF16)
    seconds = []
    for d in range(1, nx):
        seconds.append(remote(s2s, s2r.at[d - 1], t_s.at[d], t_r.at[d], across[d - 1]))
        seconds[-1].start()
    for copy in seconds:
        copy.wait()
    total = acc[pl.ds(mine0, half), :]
    for d in range(1, nx):
        total = total + s2r[d - 1].astype(F32)
    finm[...] = total.astype(BF16)
    last = remote(finm, fino, t_s.at[nx], t_r.at[nx], partner)
    last.start()

    def finish(source, row0):
        def body(q, carry):
            rows = pl.ds(pl.multiple_of(row0 + q * span, span), span)
            r = row0 // span + q
            b = bbuf[slot_ref[r]]
            upper = lax.broadcasted_iota(jnp.int32, b.shape, 0) < b.shape[0] // 2
            zero = jnp.zeros_like(b)
            maps = jnp.concatenate([jnp.where(upper, b, zero), jnp.where(upper, zero, b)], axis=1)
            low = source[pl.ds(pl.multiple_of(q * span, span), span), :]
            delta = jnp.dot(low, maps, preferred_element_type=F32)
            raw = base[rows, :]
            for d in range(1, nx):
                raw = raw + xrec[d - 1, rows, :].astype(F32)
            cos_a, sin_a = ca[pl.ds(r, 1), :], sa[pl.ds(r, 1), :]
            cos = cos_a * cb[...] - sin_a * sb[...]
            sin = sin_a * cb[...] + cos_a * sb[...]
            lane = lax.broadcasted_iota(jnp.int32, sin.shape, 1)
            sin = jnp.where(lane < 64, -sin, sin)
            for h in range(heads):
                key = raw[:, h * 256 : h * 256 + 128] + delta[:, h * 128 : (h + 1) * 128]
                value = raw[:, h * 256 + 128 : (h + 1) * 256]
                value = value + delta[:, (heads + h) * 128 : (heads + h + 1) * 128]
                out[h, 0, rows, :] = (key * cos + pltpu.roll(key, 64, 1) * sin).astype(BF16)
                out[h, 1, rows, :] = value.astype(BF16)
            return carry

        lax.fori_loop(0, half // span, body, 0)

    finish(finm, mine0)
    last.wait()
    finish(fino, other0)


def shards(hidden, base_key_value, store_a, stored_up_maps, adapter_ids, span_start):
    nw, nn = lax.axis_size("wide"), lax.axis_size("narrow")
    nx = nn // 2
    stored, features, rank_two = store_a.shape
    requests = adapter_ids.shape[0]
    tokens = hidden.shape[0]
    span = tokens // requests
    cols = base_key_value.shape[1] * 256 // nn
    owners = adapter_ids // stored
    slot_ids = adapter_ids % stored
    matches = owners[None, :] == jnp.arange(nw, dtype=jnp.int32)[:, None]
    wanted = jnp.max(jnp.where(matches, slot_ids[None, :] + 1, 0), axis=1).reshape(nw, 1)
    asked = lax.all_to_all(wanted, "wide", split_axis=0, concat_axis=0, tiled=True)
    chosen = jnp.maximum(asked[:, 0] - 1, 0)
    arrival = owners ^ lax.axis_index("wide").astype(jnp.int32)

    up = stored_up_maps.reshape(stored, rank_two, -1)
    across = up.shape[2]
    frequency = THETA ** (-(jnp.arange(64, dtype=F32) * 2.0 / 128))
    frequency = jnp.concatenate([frequency, frequency])[None, :]
    start = (span_start * span).astype(F32)[:, None] * frequency
    step = jnp.arange(span, dtype=F32)[:, None] * frequency

    vmem, smem, hbm = (pl.BlockSpec(memory_space=m) for m in (pltpu.VMEM, pltpu.SMEM, pl.ANY))
    dma = pltpu.SemaphoreType.DMA
    half = tokens // 2
    heads = cols // 256
    out = pl.pallas_call(
        functools.partial(main, nw, nx),
        out_shape=jax.ShapeDtypeStruct((heads, 2, tokens, 128), BF16),
        in_specs=[smem, smem, hbm, hbm, hbm, vmem, vmem, vmem, vmem, vmem],
        out_specs=vmem,
        scratch_shapes=[
            pltpu.VMEM((tokens, features), BF16),
            pltpu.VMEM(base_key_value.shape, BF16),
            pltpu.VMEM((features, cols), BF16),
            pltpu.VMEM(store_a.shape, BF16),
            pltpu.VMEM((nw, features, rank_two), BF16),
            pltpu.VMEM((nw, rank_two, across), BF16),
            pltpu.VMEM((nw, features, rank_two), BF16),
            pltpu.VMEM((nw, rank_two, across), BF16),
            pltpu.VMEM((nx, tokens, cols), BF16),
            pltpu.VMEM((nx, tokens, cols), BF16),
            pltpu.VMEM((nx - 1, tokens, cols), BF16),
            pltpu.VMEM((nx - 1, tokens, cols), BF16),
            pltpu.VMEM((tokens, cols), F32),
            pltpu.VMEM((tokens, rank_two), F32),
            pltpu.VMEM((half, rank_two), BF16),
            pltpu.VMEM((half, rank_two), BF16),
            pltpu.VMEM((half, rank_two), BF16),
            pltpu.VMEM((nx - 1, half, rank_two), BF16),
            pltpu.VMEM((half, rank_two), BF16),
            pltpu.VMEM((half, rank_two), BF16),
            dma((3,)), dma((nw,)), dma((nw,)), dma((nw,)), dma((nw,)),
            dma((nx,)), dma((nx,)), dma((nx,)), dma((nx,)), dma((nx + 1,)), dma((nx + 1,)),
        ],
        compiler_params=pltpu.CompilerParams(
            collective_id=0, has_side_effects=True, vmem_limit_bytes=58 * 2**20
        ),
        cost_estimate=pl.CostEstimate(
            flops=2 * tokens * features * 3072, bytes_accessed=2**25, transcendentals=0
        ),
    )(arrival, chosen, hidden, base_key_value, store_a, up, jnp.cos(start), jnp.sin(start), jnp.cos(step), jnp.sin(step))
    return out.transpose(0, 2, 1, 3)


def solution(mesh):
    placed = (
        P("wide", "narrow"),
        P("narrow", None, None, None),
        P("wide", "narrow", None),
        P("wide", None, None, "narrow", None),
        P("wide"),
        P("wide"),
    )
    return jax.shard_map(
        shards,
        mesh=mesh,
        in_specs=placed,
        out_specs=P("narrow", "wide", None, None),
        check_vma=False,
    )
```
